32 devices in a mesh: row: 4 (over y, x), col: 8 (over z, core).
Axes of the slice: x: 2, y: 2, z: 4, core: 2. Of those that a mesh axis runs over, the one named last changes fastest.
Arguments:
- amplitudes: bfloat16 [32, 256, 32, 256], P('row', None, 'col'), may hold values from -6 to 6
- factors: bfloat16 [32, 256, 384], P('row'), may hold values from -0.109375 to 0.109375
- occ_energy: float32 [32], replicated, may hold values from -2 to -0.5
- vir_energy: float32 [256], replicated, may hold values from 0.2 to 3
Outputs:
- residual: float32 [32, 256, 32, 256], P('row', None, 'col')
The draws below stay inside these ranges and needn't reach their ends.
All inputs are finite; a program needn't handle non-finite values.
Results may differ from the reference program's by a relative error of at most 0.0029.
Values may be sent and summed in bfloat16 or wider, within the bound.
A program may use at most 192 MiB of HBM per device.

```python
import math
import jax
import jax.numpy as jnp
from jax import lax

O = 32
V = 256
Q = 384


def block_scale(key, shape, shards, low, largest):
    def one(axis_at, parts):
        steps = jax.random.uniform(jax.random.fold_in(jax.random.fold_in(key, 6), axis_at), (parts,), jnp.float32, low / len(shards), largest / len(shards))
        return jnp.repeat(jnp.exp(steps), shape[axis_at] // parts).reshape((-1,) + (1,) * (len(shape) - axis_at - 1))

    factor_of = one(*shards[0])
    for cut in shards[1:]:
        factor_of = factor_of * one(*cut)
    return factor_of


def gaussian(own_key, shape, spread, limit, cuts=(), held_as=jnp.bfloat16):
    array = jax.random.normal(own_key, shape, jnp.float32) * spread
    if len(cuts) > 0:
        array = block_scale(own_key, shape, cuts, -0.22, 0.18) * array
    return jnp.clip(array, min=-limit, max=limit).astype(held_as)


def setup_inputs(seed: int = 0) -> dict:
    key_list = jax.random.split(jax.random.key(seed), 5)
    return {
        "amplitudes": gaussian(key_list[0], (O, V, O, V), 1.0, 6.0, ((0, 4), (2, 8))),
        "factors": gaussian(key_list[1], (O, V, Q), (8 * Q) ** -0.5, 0.109375, ((0, 4),)),
        "occ_energy": jnp.clip(jax.random.uniform(key_list[2], (O,), jnp.float32, -2.0, -0.5), -2.0, -0.5),
        "vir_energy": jnp.clip(jax.random.uniform(key_list[3], (V,), jnp.float32, 0.2, 3.0), 0.2, 3.0),
    }


def pair_term(left_factors, right_factors, amplitude_rows):
    left_count, virtual, auxiliary = left_factors.shape
    right_count = right_factors.shape[0]
    coulomb = jnp.dot(left_factors.reshape(left_count * virtual, auxiliary), right_factors.reshape(right_count * virtual, auxiliary).T, preferred_element_type=jnp.float32)
    exchange_part = jnp.einsum("icq,kaq->iakc", left_factors.astype(jnp.float32), right_factors.astype(jnp.float32), precision=lax.Precision.HIGHEST).reshape(left_count * virtual, right_count * virtual)
    coupling = (2.0 * coulomb - exchange_part).astype(jnp.bfloat16)
    return jnp.dot(coupling, amplitude_rows.reshape(right_count * virtual, -1), preferred_element_type=jnp.float32)


def reference(amplitudes, factors, occ_energy, vir_energy):
    group_size = math.gcd(O, 4)
    blocks = O // group_size
    factor_blocks = factors.reshape(blocks, group_size, V, Q)
    amplitude_blocks = amplitudes.reshape(blocks, group_size, V, O, V)

    def row_block(left_factors):
        def add_block(running, pieces):
            right_factors, amplitude_rows = pieces
            return running + pair_term(left_factors, right_factors, amplitude_rows), None

        start_value = jnp.zeros((group_size * V, O * V), jnp.float32)
        running, unused = lax.scan(add_block, start_value, (factor_blocks, amplitude_blocks))
        return running

    cycle_sum = lax.map(row_block, factor_blocks).reshape(O, V, O, V)
    mirrored = cycle_sum.transpose(2, 3, 0, 1)
    denominator = vir_energy[None, :, None, None] + vir_energy[None, None, None, :] - occ_energy[:, None, None, None] - occ_energy[None, None, :, None]
    return (cycle_sum + mirrored) / denominator
```

```python
import jax
import jax.numpy as jnp
from jax import lax
from jax.sharding import PartitionSpec as P

BF16 = jnp.bfloat16
F32 = jnp.float32


def denominators(occ_energy, vir_energy, rows, cols):
    row_place = lax.axis_index("row")
    col_place = lax.axis_index("col")
    occ_first = lax.dynamic_slice_in_dim(occ_energy, row_place * rows, rows, 0)
    occ_second = lax.dynamic_slice_in_dim(occ_energy, col_place * cols, cols, 0)
    return (
        vir_energy[None, :, None, None]
        + vir_energy[None, None, None, :]
        - occ_first[:, None, None, None]
        - occ_second[None, None, :, None]
    )


def coupling_of(left_one, right):
    count, virtual, _ = right.shape
    coulomb = lax.dot_general(
        left_one, right.reshape(count * virtual, -1), (((1,), (1,)), ((), ())), preferred_element_type=F32
    )
    exchange = lax.dot_general(right, left_one, (((2,), (1,)), ((), ())), preferred_element_type=F32)
    exchange = exchange.transpose(1, 0, 2).reshape(virtual, count * virtual)
    return (2.0 * coulomb - exchange).astype(BF16)


def general_body(amplitudes, factors, occ_energy, vir_energy):
    rows, virtual, cols, _ = amplitudes.shape
    all_factors = lax.all_gather(factors, "row", axis=0, tiled=True)
    all_amplitudes = lax.all_gather(amplitudes, "row", axis=0, tiled=True)
    columns = all_amplitudes.reshape(-1, cols * virtual)

    def one(left_one):
        return jnp.dot(coupling_of(left_one, all_factors), columns, preferred_element_type=F32)

    summed = lax.map(one, factors).reshape(rows, virtual, cols, virtual)
    swapped = summed.astype(BF16).transpose(2, 3, 0, 1)
    section_one = lax.all_to_all(swapped, "row", split_axis=1, concat_axis=2, tiled=True)
    section_two = lax.all_to_all(section_one, "col", split_axis=2, concat_axis=0, tiled=True)
    mirrored = lax.all_to_all(section_two, "row", split_axis=0, concat_axis=1, tiled=True)
    return (summed + mirrored) / denominators(occ_energy, vir_energy, rows, cols)


def paired_body(amplitudes, factors, occ_energy, vir_energy):
    rows, virtual, cols, _ = amplitudes.shape
    ranks = lax.axis_size("row")
    side = lax.rem(lax.axis_index("col"), 2)
    swap = [(s, s ^ 1) for s in range(2 * ranks)]
    half = rows // 2
    per = cols // ranks
    all_factors = lax.all_gather(factors, "row", axis=0, tiled=True)
    own = lax.all_to_all(amplitudes, "row", split_axis=2, concat_axis=0, tiled=True)
    own = own.reshape(-1, per * virtual)
    other = lax.ppermute(own, "col", swap)
    columns = jnp.concatenate([own, other], axis=1)
    split = all_factors.reshape(ranks, 2, half, virtual, -1)
    left = lax.dynamic_index_in_dim(split, side, 1, keepdims=False).reshape(ranks * half, virtual, -1)

    def one(left_one):
        product = jnp.dot(coupling_of(left_one, all_factors), columns, preferred_element_type=F32)
        return product.astype(BF16)

    sums = lax.map(one, left).reshape(ranks, half, virtual, 2, per, virtual)
    sums = sums.transpose(3, 0, 1, 4, 2, 5)
    direct = jnp.stack([sums[0], lax.ppermute(sums[1], "col", swap)], axis=1)
    direct = lax.all_to_all(direct, "row", split_axis=0, concat_axis=0, tiled=True)
    groups = [[2 * z + c for z in range(ranks)] for c in range(2)]
    mirror = lax.all_to_all(sums.swapaxes(0, 1), "col", split_axis=0, concat_axis=0, axis_index_groups=groups, tiled=True)
    mirror = lax.all_to_all(mirror, "row", split_axis=0, concat_axis=0, tiled=True)
    direct = direct.transpose(1, 2, 4, 0, 3, 5).reshape(2, half, virtual, cols, virtual)
    mirror = mirror.transpose(1, 0, 3, 5, 2, 4).reshape(2, half, virtual, cols, virtual)
    total = direct.astype(F32) + mirror.astype(F32)
    total = jnp.where(side == 0, total, total[::-1]).reshape(rows, virtual, cols, virtual)
    return total / denominators(occ_energy, vir_energy, rows, cols)


def solution(mesh):
    ranks, places = mesh.shape["row"], mesh.shape["col"]

    def body(amplitudes, factors, occ_energy, vir_energy):
        rows, _, cols, _ = amplitudes.shape
        paired = places == 2 * ranks and rows == 2 * cols and cols == ranks
        chosen = paired_body if paired else general_body
        return chosen(amplitudes, factors, occ_energy, vir_energy)

    in_specs = (P("row", None, "col", None), P("row", None, None), P(), P())
    out_specs = P("row", None, "col", None)
    return jax.shard_map(body, mesh=mesh, in_specs=in_specs, out_specs=out_specs, check_vma=False)
```

```python
import functools

import jax
import jax.numpy as jnp
from jax import lax
from jax.experimental import pallas as pl
from jax.experimental.pallas import tpu as pltpu
from jax.sharding import PartitionSpec as P

BF16 = jnp.bfloat16
F32 = jnp.float32


def denominators(occ_energy, vir_energy, rows, cols):
    row_place = lax.axis_index("row")
    col_place = lax.axis_index("col")
    occ_first = lax.dynamic_slice_in_dim(occ_energy, row_place * rows, rows, 0)
    occ_second = lax.dynamic_slice_in_dim(occ_energy, col_place * cols, cols, 0)
    return (
        vir_energy[None, :, None, None]
        + vir_energy[None, None, None, :]
        - occ_first[:, None, None, None]
        - occ_second[None, None, :, None]
    )


def coupling_of(left_one, right):
    count, virtual, _ = right.shape
    coulomb = lax.dot_general(
        left_one, right.reshape(count * virtual, -1), (((1,), (1,)), ((), ())), preferred_element_type=F32
    )
    exchange = lax.dot_general(right, left_one, (((2,), (1,)), ((), ())), preferred_element_type=F32)
    exchange = exchange.transpose(1, 0, 2).reshape(virtual, count * virtual)
    return (2.0 * coulomb - exchange).astype(BF16)


def general_body(amplitudes, factors, occ_energy, vir_energy):
    rows, virtual, cols, _ = amplitudes.shape
    all_factors = lax.all_gather(factors, "row", axis=0, tiled=True)
    all_amplitudes = lax.all_gather(amplitudes, "row", axis=0, tiled=True)
    columns = all_amplitudes.reshape(-1, cols * virtual)

    def one(left_one):
        return jnp.dot(coupling_of(left_one, all_factors), columns, preferred_element_type=F32)

    summed = lax.map(one, factors).reshape(rows, virtual, cols, virtual)
    swapped = summed.astype(BF16).transpose(2, 3, 0, 1)
    section_one = lax.all_to_all(swapped, "row", split_axis=1, concat_axis=2, tiled=True)
    section_two = lax.all_to_all(section_one, "col", split_axis=2, concat_axis=0, tiled=True)
    mirrored = lax.all_to_all(section_two, "row", split_axis=0, concat_axis=1, tiled=True)
    return (summed + mirrored) / denominators(occ_energy, vir_energy, rows, cols)


def coupling_block(left, right):
    wide_left = jnp.concatenate([left + left, -right], axis=1)
    wide_right = jnp.concatenate([right, left], axis=1)
    product = lax.dot_general(wide_left, wide_right, (((1,), (1,)), ((), ())), preferred_element_type=F32)
    return product.astype(BF16)


def sums_kernel(half, factors_ref, columns_ref, sums_ref, coupling, total):
    count, virtual, _ = factors_ref.shape
    depth = coupling.shape[1] // virtual
    rows = 2 * half
    side = lax.rem(lax.axis_index("col"), 2)
    pairs = count // 4

    def one_pair(pair, carry):
        group, place = pair // (half // 2), lax.rem(pair, half // 2)
        first = group * rows + side * half + 2 * place

        def one_step(step, carry):
            for u in range(2):
                left = factors_ref[first + u]
                for d in range(depth):
                    block = coupling_block(left, factors_ref[step * depth + d])
                    coupling[u * virtual:(u + 1) * virtual, d * virtual:(d + 1) * virtual] = block
            start = pl.multiple_of(step * depth * virtual, depth * virtual)
            for h in range(2):
                part = jnp.dot(coupling[...], columns_ref[h, pl.ds(start, depth * virtual), :], preferred_element_type=F32)
                total[h] = jnp.where(step == 0, part, total[h] + part)
            return carry

        lax.fori_loop(0, count // depth, one_step, 0)
        for h in range(2):
            for u in range(2):
                sums_ref[h, group, 2 * place + u] = total[h, u * virtual:(u + 1) * virtual, :].astype(BF16)
        return carry

    lax.fori_loop(0, pairs, one_pair, 0)


def pair_sums(factors, columns, half):
    count, virtual, auxiliary = factors.shape
    ranks = count // (2 * half)
    depth = 4
    vmem = pl.BlockSpec(memory_space=pltpu.VMEM)
    return pl.pallas_call(
        functools.partial(sums_kernel, half),
        out_shape=jax.ShapeDtypeStruct((2, ranks, half, virtual, virtual), BF16),
        in_specs=[vmem, vmem],
        out_specs=vmem,
        scratch_shapes=[
            pltpu.VMEM((2 * virtual, depth * virtual), BF16),
            pltpu.VMEM((2, 2 * virtual, virtual), F32),
        ],
        compiler_params=pltpu.CompilerParams(vmem_limit_bytes=48 * 1024 * 1024),
    )(factors, columns)


def paired_body(amplitudes, factors, occ_energy, vir_energy):
    rows, virtual, cols, _ = amplitudes.shape
    ranks = lax.axis_size("row")
    side = lax.rem(lax.axis_index("col"), 2)
    swap = [(s, s ^ 1) for s in range(2 * ranks)]
    half = rows // 2
    per = cols // ranks
    all_factors = lax.all_gather(factors, "row", axis=0, tiled=True)
    own = lax.all_to_all(amplitudes, "row", split_axis=2, concat_axis=0, tiled=True)
    own = own.reshape(-1, per * virtual)
    other = lax.ppermute(own, "col", swap)
    sums = pair_sums(all_factors, jnp.stack([own, other]), half)
    sums = sums.reshape(2, ranks, half, per, virtual, virtual)
    direct = jnp.stack([sums[0], lax.ppermute(sums[1], "col", swap)], axis=1)
    direct = lax.all_to_all(direct, "row", split_axis=0, concat_axis=0, tiled=True)
    groups = [[2 * z + c for z in range(ranks)] for c in range(2)]
    mirror = lax.all_to_all(sums.swapaxes(0, 1), "col", split_axis=0, concat_axis=0, axis_index_groups=groups, tiled=True)
    mirror = lax.all_to_all(mirror, "row", split_axis=0, concat_axis=0, tiled=True)
    direct = direct.transpose(1, 2, 4, 0, 3, 5).reshape(2, half, virtual, cols, virtual)
    mirror = mirror.transpose(1, 0, 3, 5, 2, 4).reshape(2, half, virtual, cols, virtual)
    total = direct.astype(F32) + mirror.astype(F32)
    total = jnp.where(side == 0, total, total[::-1]).reshape(rows, virtual, cols, virtual)
    return total / denominators(occ_energy, vir_energy, rows, cols)


def solution(mesh):
    ranks, places = mesh.shape["row"], mesh.shape["col"]

    def body(amplitudes, factors, occ_energy, vir_energy):
        rows, _, cols, _ = amplitudes.shape
        paired = places == 2 * ranks and rows == 2 * cols and cols == ranks
        chosen = paired_body if paired else general_body
        return chosen(amplitudes, factors, occ_energy, vir_energy)

    in_specs = (P("row", None, "col", None), P("row", None, None), P(), P())
    out_specs = P("row", None, "col", None)
    return jax.shard_map(body, mesh=mesh, in_specs=in_specs, out_specs=out_specs, check_vma=False)
```

```python
import functools

import jax
import jax.numpy as jnp
from jax import lax
from jax.experimental import pallas as pl
from jax.experimental.pallas import tpu as pltpu
from jax.sharding import PartitionSpec as P

BF16 = jnp.bfloat16
F32 = jnp.float32


def denominators(occ_energy, vir_energy, rows, cols):
    row_place = lax.axis_index("row")
    col_place = lax.axis_index("col")
    occ_first = lax.dynamic_slice_in_dim(occ_energy, row_place * rows, rows, 0)
    occ_second = lax.dynamic_slice_in_dim(occ_energy, col_place * cols, cols, 0)
    return (
        vir_energy[None, :, None, None]
        + vir_energy[None, None, None, :]
        - occ_first[:, None, None, None]
        - occ_second[None, None, :, None]
    )


def coupling_of(left_one, right):
    count, virtual, _ = right.shape
    coulomb = lax.dot_general(
        left_one, right.reshape(count * virtual, -1), (((1,), (1,)), ((), ())), preferred_element_type=F32
    )
    exchange = lax.dot_general(right, left_one, (((2,), (1,)), ((), ())), preferred_element_type=F32)
    exchange = exchange.transpose(1, 0, 2).reshape(virtual, count * virtual)
    return (2.0 * coulomb - exchange).astype(BF16)


def general_body(amplitudes, factors, occ_energy, vir_energy):
    rows, virtual, cols, _ = amplitudes.shape
    all_factors = lax.all_gather(factors, "row", axis=0, tiled=True)
    all_amplitudes = lax.all_gather(amplitudes, "row", axis=0, tiled=True)
    columns = all_amplitudes.reshape(-1, cols * virtual)

    def one(left_one):
        return jnp.dot(coupling_of(left_one, all_factors), columns, preferred_element_type=F32)

    summed = lax.map(one, factors).reshape(rows, virtual, cols, virtual)
    swapped = summed.astype(BF16).transpose(2, 3, 0, 1)
    section_one = lax.all_to_all(swapped, "row", split_axis=1, concat_axis=2, tiled=True)
    section_two = lax.all_to_all(section_one, "col", split_axis=2, concat_axis=0, tiled=True)
    mirrored = lax.all_to_all(section_two, "row", split_axis=0, concat_axis=1, tiled=True)
    return (summed + mirrored) / denominators(occ_energy, vir_energy, rows, cols)


def coupling_block(left, right):
    wide_left = jnp.concatenate([left + left, -right], axis=1)
    wide_right = jnp.concatenate([right, left], axis=1)
    product = lax.dot_general(wide_left, wide_right, (((1,), (1,)), ((), ())), preferred_element_type=F32)
    return product.astype(BF16)


def flip(place, offset, ranks):
    result, bit = 0, 1
    while bit < ranks:
        one, two = (place // bit) % 2, (offset // bit) % 2
        result = result + bit * (one + two - 2 * one * two)
        bit *= 2
    return result


def exchange_kernel(
    ranks, factors_ref, parts_ref, direct_ref, mirror_ref,
    held, columns, coupling, total, sums, staged,
    local_sem, factor_send, factor_recv, part_send, part_recv, pass_send, pass_recv,
    direct_send, direct_recv, stage_send, stage_recv, mirror_send, mirror_recv,
):
    rows, virtual, _ = factors_ref.shape
    half = rows // 2
    depth = coupling.shape[1] // virtual
    row = lax.axis_index("row")
    col = lax.axis_index("col")
    plane, side = col // 2, col % 2
    twin = 2 * plane + 1 - side

    def remote(src, dst, send, recv, to_row, to_col):
        return pltpu.make_async_remote_copy(
            src_ref=src, dst_ref=dst, send_sem=send, recv_sem=recv,
            device_id=(to_row, to_col), device_id_type=pl.DeviceIdType.MESH,
        )

    barrier = pltpu.get_barrier_semaphore()
    peers = [(row, twin)]
    for d in range(1, ranks):
        peers += [(flip(row, d, ranks), col), (flip(row, d, ranks), twin), (row, 2 * flip(plane, d, ranks) + side)]
    for peer in peers:
        pl.semaphore_signal(barrier, inc=1, device_id=peer, device_id_type=pl.DeviceIdType.MESH)
    pl.semaphore_wait(barrier, len(peers))

    own_half = pl.ds(side * half, half)

    def factor_copy(d):
        return remote(factors_ref.at[own_half], held.at[d, own_half], factor_send.at[d], factor_recv.at[d], flip(row, d, ranks), col)

    def part_copy(d):
        return remote(parts_ref.at[flip(row, d, ranks)], columns.at[0, d], part_send.at[d], part_recv.at[d], flip(row, d, ranks), col)

    def pass_factor(d):
        return remote(held.at[d, own_half], held.at[d, own_half], pass_send.at[0, d], pass_recv.at[0, d], row, twin)

    def pass_part(d):
        src = parts_ref.at[row] if d == 0 else columns.at[0, d]
        return remote(src, columns.at[1, d], pass_send.at[1, d], pass_recv.at[1, d], row, twin)

    def factor_other(d):
        other_half = pl.ds((1 - side) * half, half)
        return remote(held.at[d, other_half], held.at[d, other_half], pass_send.at[0, d], pass_recv.at[0, d], row, twin)

    local = [
        pltpu.make_async_copy(factors_ref, held.at[0], local_sem.at[0]),
        pltpu.make_async_copy(parts_ref.at[row], columns.at[0, 0], local_sem.at[1]),
    ]
    for copy in local:
        copy.start()
    pass_part(0).start()
    order = list(range(1, ranks))
    for group in (order[:-1], order[-1:]):
        for d in group:
            factor_copy(d).start()
        for d in group:
            part_copy(d).start()

    def direct_copy(d, h):
        to_col = col if h == 0 else twin
        return remote(sums.at[d, h], direct_ref.at[d, h], direct_send.at[d, h], direct_recv.at[d, h], flip(row, d, ranks), to_col)

    def stage_copy(d):
        goal = flip(row, d, ranks)
        slot = flip(plane, goal, ranks)
        return goal, slot, remote(sums.at[d], staged.at[slot], stage_send.at[slot], stage_recv.at[slot], row, 2 * goal + side)

    def keep_direct():
        return pltpu.make_async_copy(sums.at[0, 0], direct_ref.at[0, 0], local_sem.at[2])

    def keep_stage(d):
        return pltpu.make_async_copy(sums.at[d], staged.at[0], local_sem.at[3])

    def send_sums(d):
        for h in range(2):
            for u in range(half):
                sums[d, h, u] = total[h, d, u * virtual:(u + 1) * virtual, :].astype(BF16)
        goal, slot, copy = stage_copy(d)
        pl.when(slot != 0)(lambda: copy.start())
        pl.when(slot == 0)(lambda: keep_stage(d).start())
        for h in range(2):
            if d == 0 and h == 0:
                keep_direct().start()
            else:
                direct_copy(d, h).start()

    def tile(g, carry):
        phase = sum(jnp.where(g >= p * p, 1, 0) for p in range(1, ranks))
        n = g - phase * phase
        di = jnp.minimum(n, phase)
        dk = jnp.where(n < phase, phase, n - phase)

        @pl.when(g == 0)
        def _():
            for copy in local:
                copy.wait()
            pass_part(0).wait_recv()

        for p in range(1, ranks):
            @pl.when(g == p * p)
            def _():
                factor_copy(p).wait_recv()
                pass_factor(p).start()
                part_copy(p).wait_recv()
                pass_part(p).start()
                factor_other(p).wait_recv()
                pass_part(p).wait_recv()

        pairs, steps = half // 2, rows // depth

        def inner(m, carry):
            place, step = 2 * (m // steps), m % steps
            for u in range(2):
                left = held[di, side * half + place + u]
                for e in range(depth):
                    block = coupling_block(left, held[dk, step * depth + e])
                    coupling[u * virtual:(u + 1) * virtual, e * virtual:(e + 1) * virtual] = block
            start = pl.multiple_of(step * depth * virtual, depth * virtual)
            spot = pl.ds(pl.multiple_of(place * virtual, 2 * virtual), 2 * virtual)
            fresh = jnp.where((n == phase) & (step == 0), 1, 0)
            for h in range(2):
                part = jnp.dot(coupling[...], columns[h, dk, pl.ds(start, depth * virtual), :], preferred_element_type=F32)

                @pl.when(fresh == 1)
                def _():
                    total[h, di, spot, :] = part

                @pl.when(fresh == 0)
                def _():
                    total[h, di, spot, :] = total[h, di, spot, :] + part
            return carry

        lax.fori_loop(0, pairs * steps, inner, 0)

        last = (ranks - 1) * (ranks - 1)
        for d in range(ranks):
            @pl.when(g == (last + d if d < ranks - 1 else ranks * ranks - 1))
            def _():
                send_sums(d)
        return carry

    lax.fori_loop(0, ranks * ranks, tile, 0)

    def mirror_copy(slot, place):
        goal = flip(plane, slot, ranks)
        return remote(staged.at[slot], mirror_ref.at[place], mirror_send.at[place], mirror_recv.at[place], goal, col)

    for slot in range(ranks):
        if slot == 0:
            keep_stage(0).wait()
        else:
            remote(sums.at[0], staged.at[slot], stage_send.at[slot], stage_recv.at[slot], row, col).wait_recv()
        place = flip(row, flip(plane, slot, ranks), ranks)

        @pl.when(place != 0)
        def _():
            mirror_copy(slot, place).start()

        @pl.when(place == 0)
        def _():
            pltpu.make_async_copy(staged.at[slot], mirror_ref.at[0], local_sem.at[4]).start()

    pltpu.make_async_copy(staged.at[0], mirror_ref.at[0], local_sem.at[4]).wait()
    keep_direct().wait()
    for d in range(ranks):
        for h in range(2):
            if d > 0 or h > 0:
                direct_copy(d, h).wait()
    for d in range(1, ranks):
        factor_copy(d).wait_send()
        part_copy(d).wait_send()
        pass_factor(d).wait_send()
        remote(sums.at[0], staged.at[d], stage_send.at[d], stage_recv.at[d], row, col).wait_send()
        remote(staged.at[0], mirror_ref.at[d], mirror_send.at[d], mirror_recv.at[d], row, col).wait()
    for d in range(ranks):
        pass_part(d).wait_send()


def exchanged_sums(factors, parts):
    rows, virtual, auxiliary = factors.shape
    ranks = parts.shape[0]
    half, depth = rows // 2, rows // 2
    shape = jax.ShapeDtypeStruct((ranks, 2, half, virtual, virtual), BF16)
    anywhere = pl.BlockSpec(memory_space=pl.ANY)
    dma = pltpu.SemaphoreType.DMA
    line, square = dma((ranks,)), dma((ranks, 2))
    across = dma((2, ranks))
    return pl.pallas_call(
        functools.partial(exchange_kernel, ranks),
        out_shape=(shape, shape),
        in_specs=[anywhere, anywhere],
        out_specs=(anywhere, anywhere),
        scratch_shapes=[
            pltpu.VMEM((ranks, rows, virtual, auxiliary), BF16),
            pltpu.VMEM((2, ranks, rows * virtual, virtual), BF16),
            pltpu.VMEM((2 * virtual, depth * virtual), BF16),
            pltpu.VMEM((2, ranks, half * virtual, virtual), F32),
            pltpu.VMEM((ranks, 2, half, virtual, virtual), BF16),
            pltpu.VMEM((ranks, 2, half, virtual, virtual), BF16),
            dma((5,)), line, line, line, line, across, across, square, square, line, line, line, line,
        ],
        compiler_params=pltpu.CompilerParams(
            collective_id=0, has_side_effects=True, vmem_limit_bytes=56 * 1024 * 1024
        ),
    )(factors, parts)


def combine_kernel(ranks, place_ref, occ_ref, direct_ref, mirror_ref, vir_col_ref, vir_row_ref, out_ref):
    step = pl.program_id(0)
    row, col = place_ref[0], place_ref[1]
    cols = out_ref.shape[2]
    rows = pl.num_programs(0)
    pair_sum = vir_col_ref[...] + vir_row_ref[...]
    first = occ_ref[row * rows + step]
    for j in range(cols):
        mine = direct_ref[flip(row, j, ranks), 0, 0].astype(F32)
        turned = mirror_ref[0, 0, j].astype(F32).T
        out_ref[0, :, j, :] = (mine + turned) / (pair_sum - first - occ_ref[col * cols + j])


def combined(direct, mirror, occ_energy, vir_energy):
    ranks, _, half, virtual, _ = direct.shape
    rows = 2 * half

    def spot(step, place_ref):
        h = lax.rem(step // half + place_ref[1], 2)
        return h, lax.rem(step, half)

    def direct_map(step, place_ref, occ_ref):
        h, u = spot(step, place_ref)
        return 0, h, u, 0, 0

    def mirror_map(step, place_ref, occ_ref):
        h, q = spot(step, place_ref)
        return flip(place_ref[0], q, ranks), h, 0, 0, 0

    place = jnp.stack([lax.axis_index("row"), lax.axis_index("col")]).astype(jnp.int32)
    grid_spec = pltpu.PrefetchScalarGridSpec(
        num_scalar_prefetch=2,
        grid=(rows,),
        in_specs=[
            pl.BlockSpec((ranks, 1, 1, virtual, virtual), direct_map),
            pl.BlockSpec((1, 1, half, virtual, virtual), mirror_map),
            pl.BlockSpec((virtual, 1), lambda step, *_: (0, 0)),
            pl.BlockSpec((1, virtual), lambda step, *_: (0, 0)),
        ],
        out_specs=pl.BlockSpec((1, virtual, half, virtual), lambda step, *_: (step, 0, 0, 0)),
    )
    return pl.pallas_call(
        functools.partial(combine_kernel, ranks),
        out_shape=jax.ShapeDtypeStruct((rows, virtual, half, virtual), F32),
        grid_spec=grid_spec,
        compiler_params=pltpu.CompilerParams(vmem_limit_bytes=32 * 1024 * 1024),
    )(place, occ_energy, direct, mirror, vir_energy[:, None], vir_energy[None, :])


def paired_body(amplitudes, factors, occ_energy, vir_energy):
    rows, virtual, cols, _ = amplitudes.shape
    parts = amplitudes.transpose(2, 0, 1, 3).reshape(cols, rows * virtual, virtual)
    direct, mirror = exchanged_sums(factors, parts)
    return combined(direct, mirror, occ_energy, vir_energy)


def solution(mesh):
    ranks, places = mesh.shape["row"], mesh.shape["col"]

    def body(amplitudes, factors, occ_energy, vir_energy):
        rows, _, cols, _ = amplitudes.shape
        paired = places == 2 * ranks and rows == 2 * cols and cols == ranks and ranks in (2, 4, 8)
        chosen = paired_body if paired else general_body
        return chosen(amplitudes, factors, occ_energy, vir_energy)

    in_specs = (P("row", None, "col", None), P("row", None, None), P(), P())
    out_specs = P("row", None, "col", None)
    return jax.shard_map(body, mesh=mesh, in_specs=in_specs, out_specs=out_specs, check_vma=False)
```

```python
import functools

import jax
import jax.numpy as jnp
from jax import lax
from jax.experimental import pallas as pl
from jax.experimental.pallas import tpu as pltpu
from jax.sharding import PartitionSpec as P

BF16 = jnp.bfloat16
F32 = jnp.float32


def denominators(occ_energy, vir_energy, rows, cols):
    row_place = lax.axis_index("row")
    col_place = lax.axis_index("col")
    occ_first = lax.dynamic_slice_in_dim(occ_energy, row_place * rows, rows, 0)
    occ_second = lax.dynamic_slice_in_dim(occ_energy, col_place * cols, cols, 0)
    return (
        vir_energy[None, :, None, None]
        + vir_energy[None, None, None, :]
        - occ_first[:, None, None, None]
        - occ_second[None, None, :, None]
    )


def coupling_of(left_one, right):
    count, virtual, _ = right.shape
    coulomb = lax.dot_general(
        left_one, right.reshape(count * virtual, -1), (((1,), (1,)), ((), ())), preferred_element_type=F32
    )
    exchange = lax.dot_general(right, left_one, (((2,), (1,)), ((), ())), preferred_element_type=F32)
    exchange = exchange.transpose(1, 0, 2).reshape(virtual, count * virtual)
    return (2.0 * coulomb - exchange).astype(BF16)


def general_body(amplitudes, factors, occ_energy, vir_energy):
    rows, virtual, cols, _ = amplitudes.shape
    all_factors = lax.all_gather(factors, "row", axis=0, tiled=True)
    all_amplitudes = lax.all_gather(amplitudes, "row", axis=0, tiled=True)
    columns = all_amplitudes.reshape(-1, cols * virtual)

    def one(left_one):
        return jnp.dot(coupling_of(left_one, all_factors), columns, preferred_element_type=F32)

    summed = lax.map(one, factors).reshape(rows, virtual, cols, virtual)
    swapped = summed.astype(BF16).transpose(2, 3, 0, 1)
    section_one = lax.all_to_all(swapped, "row", split_axis=1, concat_axis=2, tiled=True)
    section_two = lax.all_to_all(section_one, "col", split_axis=2, concat_axis=0, tiled=True)
    mirrored = lax.all_to_all(section_two, "row", split_axis=0, concat_axis=1, tiled=True)
    return (summed + mirrored) / denominators(occ_energy, vir_energy, rows, cols)


def coupling_block(left, right):
    wide_left = jnp.concatenate([left + left, -right], axis=1)
    wide_right = jnp.concatenate([right, left], axis=1)
    product = lax.dot_general(wide_left, wide_right, (((1,), (1,)), ((), ())), preferred_element_type=F32)
    return product.astype(BF16)


def flip(place, offset, ranks):
    result, bit = 0, 1
    while bit < ranks:
        one, two = (place // bit) % 2, (offset // bit) % 2
        result = result + bit * (one + two - 2 * one * two)
        bit *= 2
    return result


def exchange_kernel(
    ranks, factors_ref, parts_ref, direct_ref, mirror_ref,
    held, columns, coupling, total, sums, staged,
    local_sem, factor_send, factor_recv, part_send, part_recv, pass_send, pass_recv,
    direct_send, direct_recv, stage_send, stage_recv, mirror_send, mirror_recv,
):
    rows, virtual, _ = factors_ref.shape
    half = rows // 2
    depth = coupling.shape[1] // virtual
    row = lax.axis_index("row")
    col = lax.axis_index("col")
    plane, side = col // 2, col % 2
    twin = 2 * plane + 1 - side

    def remote(src, dst, send, recv, to_row, to_col):
        return pltpu.make_async_remote_copy(
            src_ref=src, dst_ref=dst, send_sem=send, recv_sem=recv,
            device_id=(to_row, to_col), device_id_type=pl.DeviceIdType.MESH,
        )

    barrier = pltpu.get_barrier_semaphore()
    peers = [(row, twin)]
    for d in range(1, ranks):
        peers += [(flip(row, d, ranks), col), (flip(row, d, ranks), twin), (row, 2 * flip(plane, d, ranks) + side)]
    for peer in peers:
        pl.semaphore_signal(barrier, inc=1, device_id=peer, device_id_type=pl.DeviceIdType.MESH)
    pl.semaphore_wait(barrier, len(peers))

    own_half = pl.ds(side * half, half)

    def factor_copy(d):
        return remote(factors_ref.at[own_half], held.at[d, own_half], factor_send.at[d], factor_recv.at[d], flip(row, d, ranks), col)

    def part_copy(d):
        return remote(parts_ref.at[flip(row, d, ranks)], columns.at[0, d], part_send.at[d], part_recv.at[d], flip(row, d, ranks), col)

    def pass_factor(d):
        return remote(held.at[d, own_half], held.at[d, own_half], pass_send.at[0, d], pass_recv.at[0, d], row, twin)

    def pass_part(d):
        src = parts_ref.at[row] if d == 0 else columns.at[0, d]
        return remote(src, columns.at[1, d], pass_send.at[1, d], pass_recv.at[1, d], row, twin)

    def factor_other(d):
        other_half = pl.ds((1 - side) * half, half)
        return remote(held.at[d, other_half], held.at[d, other_half], pass_send.at[0, d], pass_recv.at[0, d], row, twin)

    local = [
        pltpu.make_async_copy(factors_ref, held.at[0], local_sem.at[0]),
        pltpu.make_async_copy(parts_ref.at[row], columns.at[0, 0], local_sem.at[1]),
    ]
    for copy in local:
        copy.start()
    pass_part(0).start()
    near, far = list(range(1, ranks - 1)), ranks - 1
    for d in near:
        factor_copy(d).start()

    def direct_copy(d, h):
        to_col = col if h == 0 else twin
        return remote(sums.at[d, h], direct_ref.at[d, h], direct_send.at[d, h], direct_recv.at[d, h], flip(row, d, ranks), to_col)

    def stage_copy(d, h):
        goal = flip(row, d, ranks)
        slot = flip(plane, goal, ranks)
        copy = remote(
            sums.at[d, h], staged.at[slot, h], stage_send.at[slot, h], stage_recv.at[slot, h], row, 2 * goal + side
        )
        return slot, copy

    def keep_direct():
        return pltpu.make_async_copy(sums.at[0, 0], direct_ref.at[0, 0], local_sem.at[2])

    def keep_stage(d):
        return pltpu.make_async_copy(sums.at[d], staged.at[0], local_sem.at[3])

    def send_sums(d):
        for h in range(2):
            for u in range(half):
                sums[d, h, u] = total[h, d, u * virtual:(u + 1) * virtual, :].astype(BF16)
        for h in range(2):
            slot, copy = stage_copy(d, h)
            pl.when(slot != 0)(copy.start)
        pl.when(slot == 0)(lambda: keep_stage(d).start())
        for h in range(2):
            if d == 0 and h == 0:
                keep_direct().start()
            else:
                direct_copy(d, h).start()

    base = [(di, dk) for dk in range(far) for di in range(far)]
    crossing = [(d, far) for d in near]
    closing = [(far, dk) for dk in range(ranks)]
    middle_order = base + crossing + [(0, far)] + closing
    end_order = base + [(0, far)] + closing + crossing
    at_end = jnp.where((row == 0) | (row == far), 1, 0)

    def chosen(g, which):
        result = 0
        for spot, (one, two) in enumerate(zip(end_order, middle_order)):
            value = one[which] if one[which] == two[which] else at_end * one[which] + (1 - at_end) * two[which]
            result = result + jnp.where(g == spot, value, 0)
        return result

    def tile(g, carry):
        di, dk = chosen(g, 0), chosen(g, 1)

        @pl.when(g == 0)
        def _():
            for copy in local:
                copy.wait()
            pass_part(0).wait_recv()

        @pl.when(g == 1)
        def _():
            for d in near:
                factor_copy(d).wait_send()
                part_copy(d).start()
            for d in near:
                factor_copy(d).wait_recv()
                pass_factor(d).start()

        for d in near:
            @pl.when(g == d)
            def _():
                factor_other(d).wait_recv()

        @pl.when(g == far)
        def _():
            for d in near:
                part_copy(d).wait_send()
            factor_copy(far).start()
            part_copy(far).start()
            for d in near:
                part_copy(d).wait_recv()
                pass_part(d).start()

        for d in near:
            @pl.when(g == far * d)
            def _():
                pass_part(d).wait_recv()

        @pl.when(g == far * far - 1)
        def _():
            factor_copy(far).wait_recv()
            pass_factor(far).start()
            part_copy(far).wait_recv()
            pass_part(far).start()

        @pl.when(g == far * far)
        def _():
            factor_other(far).wait_recv()
            pass_part(far).wait_recv()

        pairs, steps = half // 2, rows // depth

        def inner(m, carry):
            place, step = 2 * (m // steps), m % steps
            for u in range(2):
                left = held[di, side * half + place + u]
                for e in range(depth):
                    block = coupling_block(left, held[dk, step * depth + e])
                    coupling[u * virtual:(u + 1) * virtual, e * virtual:(e + 1) * virtual] = block
            start = pl.multiple_of(step * depth * virtual, depth * virtual)
            spot = pl.ds(pl.multiple_of(place * virtual, 2 * virtual), 2 * virtual)
            fresh = jnp.where((dk == 0) & (step == 0), 1, 0)
            for h in range(2):
                part = jnp.dot(coupling[...], columns[h, dk, pl.ds(start, depth * virtual), :], preferred_element_type=F32)

                @pl.when(fresh == 1)
                def _():
                    total[h, di, spot, :] = part

                @pl.when(fresh == 0)
                def _():
                    total[h, di, spot, :] = total[h, di, spot, :] + part
            return carry

        lax.fori_loop(0, pairs * steps, inner, 0)

        for d in range(ranks):
            ends = [max(g for g, pair in enumerate(way) if pair[0] == d) for way in (end_order, middle_order)]

            @pl.when(g == at_end * ends[0] + (1 - at_end) * ends[1])
            def _():
                send_sums(d)
        return carry

    lax.fori_loop(0, ranks * ranks, tile, 0)

    def staged_copy(slot, h):
        return remote(sums.at[0, h], staged.at[slot, h], stage_send.at[slot, h], stage_recv.at[slot, h], row, twin)

    def mirror_copy(slot, place, h, goal):
        return remote(
            staged.at[slot, h], mirror_ref.at[place, h], mirror_send.at[place, h], mirror_recv.at[place, h], goal, col
        )

    def keep_mirror(slot, h):
        return pltpu.make_async_copy(staged.at[slot, h], mirror_ref.at[0, h], local_sem.at[4 + h])

    keep_stage(0).wait()
    for slot in range(ranks):
        goal = flip(plane, slot, ranks)
        place = flip(row, goal, ranks)
        for h in range(2):
            if slot > 0:
                staged_copy(slot, h).wait_recv()
            pl.when(place != 0)(mirror_copy(slot, place, h, goal).start)
            pl.when(place == 0)(keep_mirror(slot, h).start)

    keep_direct().wait()
    for h in range(2):
        keep_mirror(0, h).wait()
        for d in range(ranks):
            if d > 0 or h > 0:
                direct_copy(d, h).wait()
            if d > 0:
                staged_copy(d, h).wait_send()
                mirror_copy(0, d, h, row).wait()
    factor_copy(far).wait_send()
    part_copy(far).wait_send()
    for d in range(ranks):
        pass_part(d).wait_send()
        if d > 0:
            pass_factor(d).wait_send()


def exchanged_sums(factors, parts):
    rows, virtual, auxiliary = factors.shape
    ranks = parts.shape[0]
    half, depth = rows // 2, rows // 2
    shape = jax.ShapeDtypeStruct((ranks, 2, half, virtual, virtual), BF16)
    anywhere = pl.BlockSpec(memory_space=pl.ANY)
    dma = pltpu.SemaphoreType.DMA
    line, square = dma((ranks,)), dma((ranks, 2))
    across = dma((2, ranks))
    return pl.pallas_call(
        functools.partial(exchange_kernel, ranks),
        out_shape=(shape, shape),
        in_specs=[anywhere, anywhere],
        out_specs=(anywhere, anywhere),
        scratch_shapes=[
            pltpu.VMEM((ranks, rows, virtual, auxiliary), BF16),
            pltpu.VMEM((2, ranks, rows * virtual, virtual), BF16),
            pltpu.VMEM((2 * virtual, depth * virtual), BF16),
            pltpu.VMEM((2, ranks, half * virtual, virtual), F32),
            pltpu.VMEM((ranks, 2, half, virtual, virtual), BF16),
            pltpu.VMEM((ranks, 2, half, virtual, virtual), BF16),
            dma((6,)), line, line, line, line, across, across, square, square, square, square, square, square,
        ],
        compiler_params=pltpu.CompilerParams(
            collective_id=0, has_side_effects=True, vmem_limit_bytes=56 * 1024 * 1024
        ),
    )(factors, parts)


def combine_kernel(ranks, place_ref, occ_ref, direct_ref, mirror_ref, vir_col_ref, vir_row_ref, out_ref):
    step = pl.program_id(0)
    row, col = place_ref[0], place_ref[1]
    cols = out_ref.shape[2]
    rows = pl.num_programs(0)
    pair_sum = vir_col_ref[...] + vir_row_ref[...]
    first = occ_ref[row * rows + step]
    for j in range(cols):
        mine = direct_ref[flip(row, j, ranks), 0, 0].astype(F32)
        turned = mirror_ref[0, 0, j].astype(F32).T
        out_ref[0, :, j, :] = (mine + turned) / (pair_sum - first - occ_ref[col * cols + j])


def combined(direct, mirror, occ_energy, vir_energy):
    ranks, _, half, virtual, _ = direct.shape
    rows = 2 * half

    def spot(step, place_ref):
        h = lax.rem(step // half + place_ref[1], 2)
        return h, lax.rem(step, half)

    def direct_map(step, place_ref, occ_ref):
        h, u = spot(step, place_ref)
        return 0, h, u, 0, 0

    def mirror_map(step, place_ref, occ_ref):
        h, q = spot(step, place_ref)
        return flip(place_ref[0], q, ranks), h, 0, 0, 0

    place = jnp.stack([lax.axis_index("row"), lax.axis_index("col")]).astype(jnp.int32)
    grid_spec = pltpu.PrefetchScalarGridSpec(
        num_scalar_prefetch=2,
        grid=(rows,),
        in_specs=[
            pl.BlockSpec((ranks, 1, 1, virtual, virtual), direct_map),
            pl.BlockSpec((1, 1, half, virtual, virtual), mirror_map),
            pl.BlockSpec((virtual, 1), lambda step, *_: (0, 0)),
            pl.BlockSpec((1, virtual), lambda step, *_: (0, 0)),
        ],
        out_specs=pl.BlockSpec((1, virtual, half, virtual), lambda step, *_: (step, 0, 0, 0)),
    )
    return pl.pallas_call(
        functools.partial(combine_kernel, ranks),
        out_shape=jax.ShapeDtypeStruct((rows, virtual, half, virtual), F32),
        grid_spec=grid_spec,
        compiler_params=pltpu.CompilerParams(vmem_limit_bytes=58 * 1024 * 1024),
    )(place, occ_energy, direct, mirror, vir_energy[:, None], vir_energy[None, :])


def paired_body(amplitudes, factors, occ_energy, vir_energy):
    rows, virtual, cols, _ = amplitudes.shape
    parts = amplitudes.transpose(2, 0, 1, 3).reshape(cols, rows * virtual, virtual)
    direct, mirror = exchanged_sums(factors, parts)
    return combined(direct, mirror, occ_energy, vir_energy)


def solution(mesh):
    ranks, places = mesh.shape["row"], mesh.shape["col"]

    def body(amplitudes, factors, occ_energy, vir_energy):
        rows, _, cols, _ = amplitudes.shape
        paired = places == 2 * ranks and rows == 2 * cols and cols == ranks and ranks in (4, 8)
        chosen = paired_body if paired else general_body
        return chosen(amplitudes, factors, occ_energy, vir_energy)

    in_specs = (P("row", None, "col", None), P("row", None, None), P(), P())
    out_specs = P("row", None, "col", None)
    return jax.shard_map(body, mesh=mesh, in_specs=in_specs, out_specs=out_specs, check_vma=False)
```

```python
import functools

import jax
import jax.numpy as jnp
from jax import lax
from jax.experimental import pallas as pl
from jax.experimental.pallas import tpu as pltpu
from jax.sharding import PartitionSpec as P

BF16 = jnp.bfloat16
F32 = jnp.float32


def denominators(occ_energy, vir_energy, rows, cols):
    row_place = lax.axis_index("row")
    col_place = lax.axis_index("col")
    occ_first = lax.dynamic_slice_in_dim(occ_energy, row_place * rows, rows, 0)
    occ_second = lax.dynamic_slice_in_dim(occ_energy, col_place * cols, cols, 0)
    return (
        vir_energy[None, :, None, None]
        + vir_energy[None, None, None, :]
        - occ_first[:, None, None, None]
        - occ_second[None, None, :, None]
    )


def coupling_of(left_one, right):
    count, virtual, _ = right.shape
    coulomb = lax.dot_general(
        left_one, right.reshape(count * virtual, -1), (((1,), (1,)), ((), ())), preferred_element_type=F32
    )
    exchange = lax.dot_general(right, left_one, (((2,), (1,)), ((), ())), preferred_element_type=F32)
    exchange = exchange.transpose(1, 0, 2).reshape(virtual, count * virtual)
    return (2.0 * coulomb - exchange).astype(BF16)


def general_body(amplitudes, factors, occ_energy, vir_energy):
    rows, virtual, cols, _ = amplitudes.shape
    all_factors = lax.all_gather(factors, "row", axis=0, tiled=True)
    all_amplitudes = lax.all_gather(amplitudes, "row", axis=0, tiled=True)
    columns = all_amplitudes.reshape(-1, cols * virtual)

    def one(left_one):
        return jnp.dot(coupling_of(left_one, all_factors), columns, preferred_element_type=F32)

    summed = lax.map(one, factors).reshape(rows, virtual, cols, virtual)
    swapped = summed.astype(BF16).transpose(2, 3, 0, 1)
    section_one = lax.all_to_all(swapped, "row", split_axis=1, concat_axis=2, tiled=True)
    section_two = lax.all_to_all(section_one, "col", split_axis=2, concat_axis=0, tiled=True)
    mirrored = lax.all_to_all(section_two, "row", split_axis=0, concat_axis=1, tiled=True)
    return (summed + mirrored) / denominators(occ_energy, vir_energy, rows, cols)


def coupling_block(left, right):
    wide_left = jnp.concatenate([left + left, -right], axis=1)
    wide_right = jnp.concatenate([right, left], axis=1)
    product = lax.dot_general(wide_left, wide_right, (((1,), (1,)), ((), ())), preferred_element_type=F32)
    return product.astype(BF16)


def flip(place, offset, ranks):
    result, bit = 0, 1
    while bit < ranks:
        one, two = (place // bit) % 2, (offset // bit) % 2
        result = result + bit * (one + two - 2 * one * two)
        bit *= 2
    return result


def exchange_kernel(
    ranks, factors_ref, parts_ref, direct_ref, mirror_ref,
    held, columns, coupling, total, sums, staged,
    local_sem, factor_send, factor_recv, part_send, part_recv, pass_send, pass_recv,
    direct_send, direct_recv, stage_send, stage_recv, mirror_send, mirror_recv,
):
    rows, virtual, _ = factors_ref.shape
    half = rows // 2
    depth = coupling.shape[1] // virtual
    row = lax.axis_index("row")
    col = lax.axis_index("col")
    plane, side = col // 2, col % 2
    twin = 2 * plane + 1 - side

    def remote(src, dst, send, recv, to_row, to_col):
        return pltpu.make_async_remote_copy(
            src_ref=src, dst_ref=dst, send_sem=send, recv_sem=recv,
            device_id=(to_row, to_col), device_id_type=pl.DeviceIdType.MESH,
        )

    barrier = pltpu.get_barrier_semaphore()
    peers = [(row, twin)]
    for d in range(1, ranks):
        peers += [(flip(row, d, ranks), col), (flip(row, d, ranks), twin), (row, 2 * flip(plane, d, ranks) + side)]
    for peer in peers:
        pl.semaphore_signal(barrier, inc=1, device_id=peer, device_id_type=pl.DeviceIdType.MESH)
    pl.semaphore_wait(barrier, len(peers))

    own_half = pl.ds(side * half, half)

    def factor_copy(d):
        return remote(factors_ref.at[own_half], held.at[d, own_half], factor_send.at[d], factor_recv.at[d], flip(row, d, ranks), col)

    def part_copy(d):
        return remote(parts_ref.at[flip(row, d, ranks)], columns.at[0, d], part_send.at[d], part_recv.at[d], flip(row, d, ranks), col)

    def pass_factor(d):
        return remote(held.at[d, own_half], held.at[d, own_half], pass_send.at[0, d], pass_recv.at[0, d], row, twin)

    def pass_part(d):
        src = parts_ref.at[row] if d == 0 else columns.at[0, d]
        return remote(src, columns.at[1, d], pass_send.at[1, d], pass_recv.at[1, d], row, twin)

    def factor_other(d):
        other_half = pl.ds((1 - side) * half, half)
        return remote(held.at[d, other_half], held.at[d, other_half], pass_send.at[0, d], pass_recv.at[0, d], row, twin)

    local = [
        pltpu.make_async_copy(factors_ref, held.at[0], local_sem.at[0]),
        pltpu.make_async_copy(parts_ref.at[row], columns.at[0, 0], local_sem.at[1]),
    ]
    for copy in local:
        copy.start()
    pass_part(0).start()
    near, far = list(range(1, ranks - 1)), ranks - 1
    turned = [side * (ranks - 1 - d) + (1 - side) * d for d in near]
    for d in turned:
        factor_copy(d).start()
    total[...] = jnp.zeros_like(total)

    def direct_copy(d, h):
        to_col = col if h == 0 else twin
        return remote(sums.at[d, h], direct_ref.at[d, h], direct_send.at[d, h], direct_recv.at[d, h], flip(row, d, ranks), to_col)

    def stage_copy(d, h):
        goal = flip(row, d, ranks)
        slot = flip(plane, goal, ranks)
        copy = remote(
            sums.at[d, h], staged.at[slot, h], stage_send.at[slot, h], stage_recv.at[slot, h], row, 2 * goal + side
        )
        return slot, copy

    def keep_direct():
        return pltpu.make_async_copy(sums.at[0, 0], direct_ref.at[0, 0], local_sem.at[2])

    def keep_stage(d):
        return pltpu.make_async_copy(sums.at[d], staged.at[0], local_sem.at[3])

    def send_sums(d):
        for h in range(2):
            for u in range(half):
                sums[d, h, u] = total[h, d, u * virtual:(u + 1) * virtual, :].astype(BF16)
        for h in range(2):
            slot, copy = stage_copy(d, h)
            pl.when(slot != 0)(copy.start)
        pl.when(slot == 0)(lambda: keep_stage(d).start())
        for h in range(2):
            if d == 0 and h == 0:
                keep_direct().start()
            else:
                direct_copy(d, h).start()

    base = [(di, dk) for dk in range(far) for di in range(far)]
    crossing = [(d, far) for d in near]
    closing = [(far, dk) for dk in range(ranks)]
    middle_order = base + crossing + [(0, far)] + closing
    end_order = base + [(0, far)] + crossing[::-1] + closing
    at_end = jnp.where((row == 0) | (row == far), 1, 0)

    def chosen(g, which):
        result = 0
        for spot, (one, two) in enumerate(zip(end_order, middle_order)):
            value = one[which] if one[which] == two[which] else at_end * one[which] + (1 - at_end) * two[which]
            result = result + jnp.where(g == spot, value, 0)
        return result

    def tile(g, carry):
        di, dk = chosen(g, 0), chosen(g, 1)

        @pl.when(g == 0)
        def _():
            for copy in local:
                copy.wait()
            pass_part(0).wait_recv()

        @pl.when(g == 1)
        def _():
            for d in turned:
                factor_copy(d).wait_send()
                part_copy(d).start()
            for d in near:
                factor_copy(d).wait_recv()
                pass_factor(d).start()

        for d in near:
            @pl.when(g == d)
            def _():
                factor_other(d).wait_recv()

        @pl.when(g == far)
        def _():
            for d in near:
                part_copy(d).wait_send()
            factor_copy(far).start()
            part_copy(far).start()
            for d in near:
                part_copy(d).wait_recv()
                pass_part(d).start()

        for d in near:
            @pl.when(g == far * d)
            def _():
                pass_part(d).wait_recv()

        @pl.when(g == far * far - 1)
        def _():
            factor_copy(far).wait_recv()
            pass_factor(far).start()
            part_copy(far).wait_recv()
            pass_part(far).start()

        @pl.when(g == far * far)
        def _():
            factor_other(far).wait_recv()
            pass_part(far).wait_recv()

        pairs, steps = half // 2, rows // depth

        def inner(m, carry):
            place, step = 2 * (m // steps), m % steps
            for u in range(2):
                left = held[di, side * half + place + u]
                for e in range(depth):
                    block = coupling_block(left, held[dk, step * depth + e])
                    coupling[u * virtual:(u + 1) * virtual, e * virtual:(e + 1) * virtual] = block
            start = pl.multiple_of(step * depth * virtual, depth * virtual)
            spot = pl.ds(pl.multiple_of(place * virtual, 2 * virtual), 2 * virtual)
            for h in range(2):
                part = jnp.dot(coupling[...], columns[h, dk, pl.ds(start, depth * virtual), :], preferred_element_type=F32)
                total[h, di, spot, :] += part
            return carry

        lax.fori_loop(0, pairs * steps, inner, 0)

        for d in range(ranks):
            ends = [max(g for g, pair in enumerate(way) if pair[0] == d) for way in (end_order, middle_order)]

            @pl.when(g == at_end * ends[0] + (1 - at_end) * ends[1])
            def _():
                send_sums(d)
        return carry

    lax.fori_loop(0, ranks * ranks, tile, 0)

    def staged_copy(slot, h):
        return remote(sums.at[0, h], staged.at[slot, h], stage_send.at[slot, h], stage_recv.at[slot, h], row, twin)

    def mirror_copy(slot, place, h, goal):
        return remote(
            staged.at[slot, h], mirror_ref.at[place, h], mirror_send.at[place, h], mirror_recv.at[place, h], goal, col
        )

    def keep_mirror(slot, h):
        return pltpu.make_async_copy(staged.at[slot, h], mirror_ref.at[0, h], local_sem.at[4 + h])

    keep_stage(0).wait()
    for slot in range(ranks):
        goal = flip(plane, slot, ranks)
        place = flip(row, goal, ranks)
        for h in range(2):
            if slot > 0:
                staged_copy(slot, h).wait_recv()
            pl.when(place != 0)(mirror_copy(slot, place, h, goal).start)
            pl.when(place == 0)(keep_mirror(slot, h).start)

    keep_direct().wait()
    for h in range(2):
        keep_mirror(0, h).wait()
        for d in range(ranks):
            if d > 0 or h > 0:
                direct_copy(d, h).wait()
            if d > 0:
                staged_copy(d, h).wait_send()
                mirror_copy(0, d, h, row).wait()
    factor_copy(far).wait_send()
    part_copy(far).wait_send()
    for d in range(ranks):
        pass_part(d).wait_send()
        if d > 0:
            pass_factor(d).wait_send()


def exchanged_sums(factors, parts):
    rows, virtual, auxiliary = factors.shape
    ranks = parts.shape[0]
    half, depth = rows // 2, rows // 2
    shape = jax.ShapeDtypeStruct((ranks, 2, half, virtual, virtual), BF16)
    anywhere = pl.BlockSpec(memory_space=pl.ANY)
    dma = pltpu.SemaphoreType.DMA
    line, square = dma((ranks,)), dma((ranks, 2))
    across = dma((2, ranks))
    return pl.pallas_call(
        functools.partial(exchange_kernel, ranks),
        out_shape=(shape, shape),
        in_specs=[anywhere, anywhere],
        out_specs=(anywhere, anywhere),
        scratch_shapes=[
            pltpu.VMEM((ranks, rows, virtual, auxiliary), BF16),
            pltpu.VMEM((2, ranks, rows * virtual, virtual), BF16),
            pltpu.VMEM((2 * virtual, depth * virtual), BF16),
            pltpu.VMEM((2, ranks, half * virtual, virtual), F32),
            pltpu.VMEM((ranks, 2, half, virtual, virtual), BF16),
            pltpu.VMEM((ranks, 2, half, virtual, virtual), BF16),
            dma((6,)), line, line, line, line, across, across, square, square, square, square, square, square,
        ],
        compiler_params=pltpu.CompilerParams(
            collective_id=0, has_side_effects=True, vmem_limit_bytes=56 * 1024 * 1024
        ),
    )(factors, parts)


def combine_kernel(ranks, place_ref, occ_ref, direct_ref, mirror_ref, vir_col_ref, vir_row_ref, out_ref):
    step = pl.program_id(0)
    row, col = place_ref[0], place_ref[1]
    cols = out_ref.shape[2]
    rows = pl.num_programs(0)
    pair_sum = vir_col_ref[...] + vir_row_ref[...]
    first = occ_ref[row * rows + step]
    for j in range(cols):
        mine = direct_ref[flip(row, j, ranks), 0, 0].astype(F32)
        turned = mirror_ref[0, 0, j].astype(F32).T
        out_ref[0, :, j, :] = (mine + turned) / (pair_sum - first - occ_ref[col * cols + j])


def combined(direct, mirror, occ_energy, vir_energy):
    ranks, _, half, virtual, _ = direct.shape
    rows = 2 * half

    def spot(step, place_ref):
        h = lax.rem(step // half + place_ref[1], 2)
        return h, lax.rem(step, half)

    def direct_map(step, place_ref, occ_ref):
        h, u = spot(step, place_ref)
        return 0, h, u, 0, 0

    def mirror_map(step, place_ref, occ_ref):
        h, q = spot(step, place_ref)
        return flip(place_ref[0], q, ranks), h, 0, 0, 0

    place = jnp.stack([lax.axis_index("row"), lax.axis_index("col")]).astype(jnp.int32)
    grid_spec = pltpu.PrefetchScalarGridSpec(
        num_scalar_prefetch=2,
        grid=(rows,),
        in_specs=[
            pl.BlockSpec((ranks, 1, 1, virtual, virtual), direct_map),
            pl.BlockSpec((1, 1, half, virtual, virtual), mirror_map),
            pl.BlockSpec((virtual, 1), lambda step, *_: (0, 0)),
            pl.BlockSpec((1, virtual), lambda step, *_: (0, 0)),
        ],
        out_specs=pl.BlockSpec((1, virtual, half, virtual), lambda step, *_: (step, 0, 0, 0)),
    )
    return pl.pallas_call(
        functools.partial(combine_kernel, ranks),
        out_shape=jax.ShapeDtypeStruct((rows, virtual, half, virtual), F32),
        grid_spec=grid_spec,
        compiler_params=pltpu.CompilerParams(vmem_limit_bytes=58 * 1024 * 1024),
    )(place, occ_energy, direct, mirror, vir_energy[:, None], vir_energy[None, :])


def paired_body(amplitudes, factors, occ_energy, vir_energy):
    rows, virtual, cols, _ = amplitudes.shape
    parts = amplitudes.transpose(2, 0, 1, 3).reshape(cols, rows * virtual, virtual)
    direct, mirror = exchanged_sums(factors, parts)
    return combined(direct, mirror, occ_energy, vir_energy)


def solution(mesh):
    ranks, places = mesh.shape["row"], mesh.shape["col"]

    def body(amplitudes, factors, occ_energy, vir_energy):
        rows, _, cols, _ = amplitudes.shape
        paired = places == 2 * ranks and rows == 2 * cols and cols == ranks and ranks in (4, 8)
        chosen = paired_body if paired else general_body
        return chosen(amplitudes, factors, occ_energy, vir_energy)

    in_specs = (P("row", None, "col", None), P("row", None, None), P(), P())
    out_specs = P("row", None, "col", None)
    return jax.shard_map(body, mesh=mesh, in_specs=in_specs, out_specs=out_specs, check_vma=False)
```

```python
import functools

import jax
import jax.numpy as jnp
from jax import lax
from jax.experimental import pallas as pl
from jax.experimental.pallas import tpu as pltpu
from jax.sharding import PartitionSpec as P

BF16 = jnp.bfloat16
F32 = jnp.float32


def denominators(occ_energy, vir_energy, rows, cols):
    row_place = lax.axis_index("row")
    col_place = lax.axis_index("col")
    occ_first = lax.dynamic_slice_in_dim(occ_energy, row_place * rows, rows, 0)
    occ_second = lax.dynamic_slice_in_dim(occ_energy, col_place * cols, cols, 0)
    return (
        vir_energy[None, :, None, None]
        + vir_energy[None, None, None, :]
        - occ_first[:, None, None, None]
        - occ_second[None, None, :, None]
    )


def coupling_of(left_one, right):
    count, virtual, _ = right.shape
    coulomb = lax.dot_general(
        left_one, right.reshape(count * virtual, -1), (((1,), (1,)), ((), ())), preferred_element_type=F32
    )
    exchange = lax.dot_general(right, left_one, (((2,), (1,)), ((), ())), preferred_element_type=F32)
    exchange = exchange.transpose(1, 0, 2).reshape(virtual, count * virtual)
    return (2.0 * coulomb - exchange).astype(BF16)


def general_body(amplitudes, factors, occ_energy, vir_energy):
    rows, virtual, cols, _ = amplitudes.shape
    all_factors = lax.all_gather(factors, "row", axis=0, tiled=True)
    all_amplitudes = lax.all_gather(amplitudes, "row", axis=0, tiled=True)
    columns = all_amplitudes.reshape(-1, cols * virtual)

    def one(left_one):
        return jnp.dot(coupling_of(left_one, all_factors), columns, preferred_element_type=F32)

    summed = lax.map(one, factors).reshape(rows, virtual, cols, virtual)
    swapped = summed.astype(BF16).transpose(2, 3, 0, 1)
    section_one = lax.all_to_all(swapped, "row", split_axis=1, concat_axis=2, tiled=True)
    section_two = lax.all_to_all(section_one, "col", split_axis=2, concat_axis=0, tiled=True)
    mirrored = lax.all_to_all(section_two, "row", split_axis=0, concat_axis=1, tiled=True)
    return (summed + mirrored) / denominators(occ_energy, vir_energy, rows, cols)


def coupling_block(left, right):
    wide_left = jnp.concatenate([left + left, -right], axis=1)
    wide_right = jnp.concatenate([right, left], axis=1)
    product = lax.dot_general(wide_left, wide_right, (((1,), (1,)), ((), ())), preferred_element_type=F32)
    return product.astype(BF16)


def flip(place, offset, ranks):
    result, bit = 0, 1
    while bit < ranks:
        one, two = (place // bit) % 2, (offset // bit) % 2
        result = result + bit * (one + two - 2 * one * two)
        bit *= 2
    return result


def exchange_kernel(
    ranks, factors_ref, parts_ref, direct_ref, mirror_ref,
    held, columns, coupling, total, sums, staged,
    local_sem, factor_send, factor_recv, part_send, part_recv, pass_send, pass_recv,
    direct_send, direct_recv, stage_send, stage_recv, mirror_send, mirror_recv,
):
    rows, virtual, _ = factors_ref.shape
    half = rows // 2
    depth = coupling.shape[1] // virtual
    row = lax.axis_index("row")
    col = lax.axis_index("col")
    plane, side = col // 2, col % 2
    twin = 2 * plane + 1 - side

    def remote(src, dst, send, recv, to_row, to_col):
        return pltpu.make_async_remote_copy(
            src_ref=src, dst_ref=dst, send_sem=send, recv_sem=recv,
            device_id=(to_row, to_col), device_id_type=pl.DeviceIdType.MESH,
        )

    barrier = pltpu.get_barrier_semaphore()
    peers = [(row, twin)]
    for d in range(1, ranks):
        peers += [(flip(row, d, ranks), col), (flip(row, d, ranks), twin), (row, 2 * flip(plane, d, ranks) + side)]
    for peer in peers:
        pl.semaphore_signal(barrier, inc=1, device_id=peer, device_id_type=pl.DeviceIdType.MESH)
    pl.semaphore_wait(barrier, len(peers))

    own_half = pl.ds(side * half, half)

    def factor_copy(d):
        return remote(factors_ref.at[own_half], held.at[d, own_half], factor_send.at[d], factor_recv.at[d], flip(row, d, ranks), col)

    def part_copy(d):
        return remote(parts_ref.at[flip(row, d, ranks)], columns.at[0, d], part_send.at[d], part_recv.at[d], flip(row, d, ranks), col)

    def pass_factor(d):
        return remote(held.at[d, own_half], held.at[d, own_half], pass_send.at[0, d], pass_recv.at[0, d], row, twin)

    def pass_part(d):
        src = parts_ref.at[row] if d == 0 else columns.at[0, d]
        return remote(src, columns.at[1, d], pass_send.at[1, d], pass_recv.at[1, d], row, twin)

    def factor_other(d):
        other_half = pl.ds((1 - side) * half, half)
        return remote(held.at[d, other_half], held.at[d, other_half], pass_send.at[0, d], pass_recv.at[0, d], row, twin)

    local = [
        pltpu.make_async_copy(factors_ref, held.at[0], local_sem.at[0]),
        pltpu.make_async_copy(parts_ref.at[row], columns.at[0, 0], local_sem.at[1]),
    ]
    for copy in local:
        copy.start()
    pass_part(0).start()
    near, far = list(range(1, ranks - 1)), ranks - 1
    turned = [side * (ranks - 1 - d) + (1 - side) * d for d in near]
    for d in turned:
        factor_copy(d).start()
    total[...] = jnp.zeros_like(total)

    def direct_copy(d, h):
        to_col = col if h == 0 else twin
        return remote(sums.at[d, h], direct_ref.at[d, h], direct_send.at[d, h], direct_recv.at[d, h], flip(row, d, ranks), to_col)

    def stage_copy(d, h):
        goal = flip(row, d, ranks)
        slot = flip(plane, goal, ranks)
        copy = remote(
            sums.at[d, h], staged.at[slot, h], stage_send.at[slot, h], stage_recv.at[slot, h], row, 2 * goal + side
        )
        return slot, copy

    def keep_direct():
        return pltpu.make_async_copy(sums.at[0, 0], direct_ref.at[0, 0], local_sem.at[2])

    def keep_stage(d):
        return pltpu.make_async_copy(sums.at[d], staged.at[0], local_sem.at[3])

    def send_sums(d):
        for h in range(2):
            for u in range(half):
                sums[d, h, u] = total[h, d, u * virtual:(u + 1) * virtual, :].astype(BF16)
        for h in range(2):
            slot, copy = stage_copy(d, h)
            pl.when(slot != 0)(copy.start)
        pl.when(slot == 0)(lambda: keep_stage(d).start())
        for h in range(2):
            if d == 0 and h == 0:
                keep_direct().start()
            else:
                direct_copy(d, h).start()

    base = [(di, dk) for dk in range(far) for di in range(far)]
    crossing = [(d, far) for d in near]
    closing = [(far, dk) for dk in range(ranks)]
    middle_order = base + crossing + [(0, far)] + closing
    end_order = base + [(0, far), crossing[-1]] + closing + crossing[:-1]
    at_end = jnp.where((row == 0) | (row == far), 1, 0)

    def chosen(g, which):
        result = 0
        for spot, (one, two) in enumerate(zip(end_order, middle_order)):
            value = one[which] if one[which] == two[which] else at_end * one[which] + (1 - at_end) * two[which]
            result = result + jnp.where(g == spot, value, 0)
        return result

    def tile(g, carry):
        di, dk = chosen(g, 0), chosen(g, 1)

        @pl.when(g == 0)
        def _():
            for copy in local:
                copy.wait()
            pass_part(0).wait_recv()

        @pl.when(g == 1)
        def _():
            for d in turned:
                factor_copy(d).wait_send()
                part_copy(d).start()
            for d in near:
                factor_copy(d).wait_recv()
                pass_factor(d).start()

        for d in near:
            @pl.when(g == d)
            def _():
                factor_other(d).wait_recv()

        @pl.when(g == far)
        def _():
            for d in near:
                part_copy(d).wait_send()
            factor_copy(far).start()
            part_copy(far).start()
            for d in near:
                part_copy(d).wait_recv()
                pass_part(d).start()

        for d in near:
            @pl.when(g == far * d)
            def _():
                pass_part(d).wait_recv()

        @pl.when(g == far * far - 1)
        def _():
            factor_copy(far).wait_recv()
            pass_factor(far).start()
            part_copy(far).wait_recv()
            pass_part(far).start()

        @pl.when(g == far * far)
        def _():
            factor_other(far).wait_recv()
            pass_part(far).wait_recv()

        def inner(step, carry):
            for u in range(half):
                left = held[di, side * half + u]
                for e in range(depth):
                    block = coupling_block(left, held[dk, step * depth + e])
                    coupling[u * virtual:(u + 1) * virtual, e * virtual:(e + 1) * virtual] = block
            start = pl.multiple_of(step * depth * virtual, depth * virtual)
            for h in range(2):
                part = jnp.dot(coupling[...], columns[h, dk, pl.ds(start, depth * virtual), :], preferred_element_type=F32)
                total[h, di] += part
            return carry

        lax.fori_loop(0, rows // depth, inner, 0)

        for d in range(ranks):
            ends = [max(g for g, pair in enumerate(way) if pair[0] == d) for way in (end_order, middle_order)]

            @pl.when(g == at_end * ends[0] + (1 - at_end) * ends[1])
            def _():
                send_sums(d)
        return carry

    lax.fori_loop(0, ranks * ranks, tile, 0)

    def staged_copy(slot, h):
        return remote(sums.at[0, h], staged.at[slot, h], stage_send.at[slot, h], stage_recv.at[slot, h], row, twin)

    def mirror_copy(slot, place, h, goal):
        return remote(
            staged.at[slot, h], mirror_ref.at[place, h], mirror_send.at[place, h], mirror_recv.at[place, h], goal, col
        )

    def keep_mirror(slot, h):
        return pltpu.make_async_copy(staged.at[slot, h], mirror_ref.at[0, h], local_sem.at[4 + h])

    keep_stage(0).wait()
    for slot in range(ranks):
        goal = flip(plane, slot, ranks)
        place = flip(row, goal, ranks)
        for h in range(2):
            if slot > 0:
                staged_copy(slot, h).wait_recv()
            pl.when(place != 0)(mirror_copy(slot, place, h, goal).start)
            pl.when(place == 0)(keep_mirror(slot, h).start)

    keep_direct().wait()
    for h in range(2):
        keep_mirror(0, h).wait()
        for d in range(ranks):
            if d > 0 or h > 0:
                direct_copy(d, h).wait()
            if d > 0:
                staged_copy(d, h).wait_send()
                mirror_copy(0, d, h, row).wait()
    factor_copy(far).wait_send()
    part_copy(far).wait_send()
    for d in range(ranks):
        pass_part(d).wait_send()
        if d > 0:
            pass_factor(d).wait_send()


def exchanged_sums(factors, parts):
    rows, virtual, auxiliary = factors.shape
    ranks = parts.shape[0]
    half, depth = rows // 2, rows // 2
    shape = jax.ShapeDtypeStruct((ranks, 2, half, virtual, virtual), BF16)
    anywhere = pl.BlockSpec(memory_space=pl.ANY)
    dma = pltpu.SemaphoreType.DMA
    line, square = dma((ranks,)), dma((ranks, 2))
    across = dma((2, ranks))
    return pl.pallas_call(
        functools.partial(exchange_kernel, ranks),
        out_shape=(shape, shape),
        in_specs=[anywhere, anywhere],
        out_specs=(anywhere, anywhere),
        scratch_shapes=[
            pltpu.VMEM((ranks, rows, virtual, auxiliary), BF16),
            pltpu.VMEM((2, ranks, rows * virtual, virtual), BF16),
            pltpu.VMEM((half * virtual, depth * virtual), BF16),
            pltpu.VMEM((2, ranks, half * virtual, virtual), F32),
            pltpu.VMEM((ranks, 2, half, virtual, virtual), BF16),
            pltpu.VMEM((ranks, 2, half, virtual, virtual), BF16),
            dma((6,)), line, line, line, line, across, across, square, square, square, square, square, square,
        ],
        compiler_params=pltpu.CompilerParams(
            collective_id=0, has_side_effects=True, vmem_limit_bytes=56 * 1024 * 1024
        ),
    )(factors, parts)


def combine_kernel(ranks, place_ref, occ_ref, direct_ref, mirror_ref, vir_col_ref, vir_row_ref, out_ref):
    step = pl.program_id(0)
    row, col = place_ref[0], place_ref[1]
    cols = out_ref.shape[2]
    rows = pl.num_programs(0)
    pair_sum = vir_col_ref[...] + vir_row_ref[...]
    first = occ_ref[row * rows + step]
    for j in range(cols):
        mine = direct_ref[flip(row, j, ranks), 0, 0].astype(F32)
        turned = mirror_ref[0, 0, j].T.astype(F32)
        out_ref[0, :, j, :] = (mine + turned) / (pair_sum - first - occ_ref[col * cols + j])


def combined(direct, mirror, occ_energy, vir_energy):
    ranks, _, half, virtual, _ = direct.shape
    rows = 2 * half

    def spot(step, place_ref):
        h = lax.rem(step // half + place_ref[1], 2)
        return h, lax.rem(step, half)

    def direct_map(step, place_ref, occ_ref):
        h, u = spot(step, place_ref)
        return 0, h, u, 0, 0

    def mirror_map(step, place_ref, occ_ref):
        h, q = spot(step, place_ref)
        return flip(place_ref[0], q, ranks), h, 0, 0, 0

    place = jnp.stack([lax.axis_index("row"), lax.axis_index("col")]).astype(jnp.int32)
    grid_spec = pltpu.PrefetchScalarGridSpec(
        num_scalar_prefetch=2,
        grid=(rows,),
        in_specs=[
            pl.BlockSpec((ranks, 1, 1, virtual, virtual), direct_map),
            pl.BlockSpec((1, 1, half, virtual, virtual), mirror_map),
            pl.BlockSpec((virtual, 1), lambda step, *_: (0, 0)),
            pl.BlockSpec((1, virtual), lambda step, *_: (0, 0)),
        ],
        out_specs=pl.BlockSpec((1, virtual, half, virtual), lambda step, *_: (step, 0, 0, 0)),
    )
    return pl.pallas_call(
        functools.partial(combine_kernel, ranks),
        out_shape=jax.ShapeDtypeStruct((rows, virtual, half, virtual), F32),
        grid_spec=grid_spec,
        compiler_params=pltpu.CompilerParams(vmem_limit_bytes=58 * 1024 * 1024),
    )(place, occ_energy, direct, mirror, vir_energy[:, None], vir_energy[None, :])


def paired_body(amplitudes, factors, occ_energy, vir_energy):
    rows, virtual, cols, _ = amplitudes.shape
    parts = amplitudes.transpose(2, 0, 1, 3).reshape(cols, rows * virtual, virtual)
    direct, mirror = exchanged_sums(factors, parts)
    return combined(direct, mirror, occ_energy, vir_energy)


def solution(mesh):
    ranks, places = mesh.shape["row"], mesh.shape["col"]

    def body(amplitudes, factors, occ_energy, vir_energy):
        rows, _, cols, _ = amplitudes.shape
        paired = places == 2 * ranks and rows == 2 * cols and cols == ranks and ranks in (4, 8)
        chosen = paired_body if paired else general_body
        return chosen(amplitudes, factors, occ_energy, vir_energy)

    in_specs = (P("row", None, "col", None), P("row", None, None), P(), P())
    out_specs = P("row", None, "col", None)
    return jax.shard_map(body, mesh=mesh, in_specs=in_specs, out_specs=out_specs, check_vma=False)
```
